32 devices in a mesh: grp: 2 (over y), ep: 8 (over z, x), tp: 2 (over core).
Axes of the slice: x: 2, y: 2, z: 4, core: 2. Of those that a mesh axis runs over, the one named last changes fastest.
Arguments:
- cotangent: bfloat16 [2048, 3584], P(('grp', 'ep'), 'tp'), parts along dimension 0, may hold values from -1.5 to 1.5
- gate_weights: bfloat16 [2048, 8], P(('grp', 'ep')), parts along dimension 0, may hold values from 0.099609375 to 2
- expert_ids: int32 [2048, 8], P(('grp', 'ep')), parts along dimension 0, may hold values from 0 to 15, as said below
- slot_ids: int32 [2048, 8], P(('grp', 'ep')), parts along dimension 0, may hold values from 0 to 65, as said below
- pre_acts: bfloat16 [16, 1056, 2, 1024], P('ep', 'grp', None, 'tp'), parts along dimension 1, may hold values from -6 to 6
- w_down: bfloat16 [16, 1024, 3584], P('ep', 'tp'), may hold values from -0.1875 to 0.1875
Outputs:
- grad_pre: bfloat16 [16, 1056, 2, 1024], P('ep', 'grp', None, 'tp'), parts along dimension 1
- grad_gates: float32 [2048, 8], P(('grp', 'ep')), parts along dimension 0
The draws below stay inside these ranges and needn't reach their ends.
There are 2 independent parts, one for each index of `grp`. The reference program is written for one: setup_inputs(seed, part) draws one part's arguments, and reference() takes and returns one part's arrays. A program takes and returns all parts, laid end to end along the dimension named above; an argument that names none is the same for every part. Nothing has to cross between parts.
Inputs may be any that keep to these rules, and one draw needn't show every extreme that they name: `expert_ids`: each token names 8 different experts; the rows of one index of ep name no expert more than 66 times, and some expert is named exactly 66 times by the rows of every index of ep. `slot_ids`: for each index of ep and each expert, the choices that name that expert have distinct positions.
All inputs are finite; a program needn't handle non-finite values.
Results may differ from the reference program's by a relative error of at most 0.001.
Values may be sent and summed in bfloat16 or wider, within the bound.
A program may use at most 128 MiB of HBM per device.

```python
import math
import jax
import jax.numpy as jnp
from jax import lax

D = 3584
HID = 1024
TOP = 8
TOK_DEV = 128
EXPERTS = 16
TOKENS = 1024
CAP = 66
SLOTS = 528
N_EP = 8


def shuffled(keys, length):

    def one_row(one_key):
        return jax.random.permutation(one_key, length)
    return jax.vmap(one_row)(keys)


def route_table(key):
    base_count = EXPERTS // TOP
    average = TOK_DEV // base_count
    key_count, key_order, key_label, key_full, key_offset = jax.random.split(key, 5)
    amount = jax.random.randint(key_count, (N_EP, base_count // 2), 0, 3).astype(jnp.int32)
    amount = amount.at[:, 0].set(2)
    counts = average + jnp.stack([amount, -amount], axis=2).reshape(N_EP, base_count)
    bounds = jnp.cumsum(counts, axis=1)
    positions = jnp.arange(TOK_DEV, dtype=jnp.int32)
    sorted_base = jnp.sum((positions[None, :, None] >= bounds[:, None, :]).astype(jnp.int32), axis=2)
    orders = shuffled(jax.random.split(key_order, N_EP), TOK_DEV)
    base_of = jnp.take_along_axis(sorted_base, orders, axis=1)
    labels = base_of[:, :, None] + base_count * jnp.arange(TOP, dtype=jnp.int32)[None, None, :]
    flat_labels = labels.reshape(N_EP, TOK_DEV * TOP)
    relabel = shuffled(jax.random.split(key_label, N_EP), EXPERTS).astype(jnp.int32)
    full_expert = jax.random.randint(key_full, (), 0, EXPERTS).astype(jnp.int32)
    mapped = jnp.take_along_axis(relabel, flat_labels, axis=1).reshape(N_EP, TOK_DEV, TOP)
    experts = (mapped - relabel[:, :1, None] + full_expert) % EXPERTS
    onehot = (base_of[:, :, None] == jnp.arange(base_count, dtype=jnp.int32)[None, None, :]).astype(jnp.int32)
    running = jnp.cumsum(onehot, axis=1)
    rank_in = jnp.take_along_axis(running, base_of[:, :, None], axis=2)[:, :, 0] - 1
    offsets = jax.random.randint(key_offset, (N_EP, EXPERTS), 0, CAP).astype(jnp.int32)
    offset = jnp.take_along_axis(offsets, flat_labels, axis=1).reshape(N_EP, TOK_DEV, TOP)
    slot_of = (rank_in[:, :, None] + offset) % CAP
    return (experts.reshape(TOKENS, TOP).astype(jnp.int32), slot_of.reshape(TOKENS, TOP).astype(jnp.int32))


def draw_expert_ids(key, part):
    return route_table(key)[0]


def draw_slot_ids(key, part):
    return route_table(key)[1]


def levels(key, shape, cuts, least, top_value):
    def one(position, blocks):
        heights = jax.random.uniform(jax.random.fold_in(jax.random.fold_in(key, 6), position), (blocks,), jnp.float32, least / len(cuts), top_value / len(cuts))
        return jnp.repeat(jnp.exp(heights), shape[position] // blocks).reshape((-1,) + (1,) * (len(shape) - position - 1))

    loudness = one(*cuts[0])
    for cut in cuts[1:]:
        loudness = loudness * one(*cut)
    return loudness


def scatter_about(stream_key, shape, spread, bound, pieces=(), kind=jnp.bfloat16):
    entries = spread * jax.random.normal(stream_key, shape, jnp.float32)
    if pieces:
        entries = entries * levels(stream_key, shape, pieces, -0.22, 0.18)
    return jnp.clip(entries, -bound, bound).astype(kind)


def setup_inputs(seed: int = 0, part: int = 0) -> dict:
    seeds = jax.random.split(jax.random.key(seed), 7)
    part_keys = jax.random.split(jax.random.fold_in(seeds[6], part), 7)
    return {
        "cotangent": scatter_about(part_keys[0], (TOKENS, D), 0.25, 1.5, ((0, 8), (1, 2))),
        "gate_weights": jnp.clip(jnp.exp(math.log(2.0) - 2.9996462 * jax.random.uniform(part_keys[1], (TOKENS, TOP), jnp.float32) ** levels(part_keys[1], (TOKENS, TOP), ((0, 8),), -0.2, 0.2)), 0.099609375, 2.0).astype(jnp.bfloat16),
        "expert_ids": draw_expert_ids(jax.random.fold_in(jax.random.fold_in(seeds[6], part), 71), part),
        "slot_ids": draw_slot_ids(jax.random.fold_in(jax.random.fold_in(seeds[6], part), 71), part),
        "pre_acts": scatter_about(part_keys[4], (EXPERTS, SLOTS, 2, HID), 1.0, 6.0, ((0, 8), (3, 2))),
        "w_down": scatter_about(seeds[5], (EXPERTS, HID, D), HID ** -0.5, 0.1875, ((0, 8), (1, 2))),
    }


def reference(cotangent, gate_weights, expert_ids, slot_ids, pre_acts, w_down):
    source = (jnp.arange(TOKENS, dtype=jnp.int32) // TOK_DEV)[:, None]
    target = (expert_ids * SLOTS + source * CAP + slot_ids).astype(jnp.int32)
    pair_index = jnp.arange(TOKENS * TOP, dtype=jnp.int32)
    filler = jnp.full((EXPERTS * SLOTS,), TOKENS * TOP, jnp.int32).at[target.reshape(-1)].set(pair_index)
    filler = filler.reshape(EXPERTS, SLOTS)
    padded_rows = jnp.concatenate([cotangent, jnp.zeros((1, D), cotangent.dtype)], axis=0)
    padded_gate = jnp.concatenate([gate_weights.reshape(-1), jnp.zeros((1,), gate_weights.dtype)], axis=0)

    def one_expert(operands):
        filled, saved, weight = operands
        matrix = padded_rows[filled // TOP]
        gate_rows = padded_gate[filled].astype(jnp.float32)
        grad_hidden = jnp.dot(matrix, weight.T, preferred_element_type=jnp.float32)
        gate_pre = saved[:, 0].astype(jnp.float32)
        up_pre = saved[:, 1].astype(jnp.float32)
        sigmoid_gate = jax.nn.sigmoid(gate_pre)
        activated = gate_pre * sigmoid_gate
        slot_grad = jnp.sum(activated * up_pre * grad_hidden, axis=1)
        scaled = gate_rows[:, None] * grad_hidden
        grad_gate = scaled * up_pre * sigmoid_gate * (1.0 + gate_pre * (1.0 - sigmoid_gate))
        grad_up = scaled * activated
        return jnp.stack([grad_gate, grad_up], axis=1).astype(jnp.bfloat16), slot_grad

    grad_pre, slot_grads = lax.map(one_expert, (filler, pre_acts, w_down))
    grad_gates = slot_grads.reshape(-1)[target]
    return grad_pre, grad_gates
```

```python
import functools

import jax
import jax.numpy as jnp
from jax import lax
from jax.experimental import pallas as pl
from jax.experimental.pallas import tpu as pltpu
from jax.sharding import PartitionSpec as P

MESH = pl.DeviceIdType.MESH
KC = 256
NZ, NX = 4, 2


def slotted(cotangent, gate_weights, expert_ids, slot_ids, pre_acts, w_down):
    peers = lax.axis_size("ep")
    tok_rows, chosen = expert_ids.shape
    experts_here = w_down.shape[0]
    slot_rows = pre_acts.shape[1]
    capacity = slot_rows // peers
    owners = expert_ids // experts_here
    target_slot = expert_ids % experts_here * slot_rows + owners * capacity + slot_ids
    pair_index = jnp.arange(tok_rows * chosen, dtype=jnp.int32)
    filler = (
        jnp.full((experts_here * slot_rows,), tok_rows * chosen, jnp.int32)
        .at[target_slot.reshape(-1)]
        .set(pair_index)
    )
    padded_gate = jnp.concatenate(
        [gate_weights.reshape(-1), jnp.zeros((1,), gate_weights.dtype)], axis=0
    )
    send_gate = padded_gate[filler].reshape(experts_here, peers, capacity)
    padded = jnp.concatenate(
        [cotangent, jnp.zeros((1, cotangent.shape[1]), cotangent.dtype)], axis=0
    )
    half_rows = lax.all_to_all(
        padded[filler // chosen].reshape(experts_here, peers, capacity, cotangent.shape[1]),
        "ep",
        split_axis=1,
        concat_axis=1,
        tiled=True,
    )
    arrived_gate = lax.all_to_all(send_gate, "ep", split_axis=1, concat_axis=1, tiled=True)
    arrived = lax.all_gather(half_rows, "tp", axis=3, tiled=True)
    arrived = arrived.reshape(experts_here, slot_rows, arrived.shape[3])
    gate_rows = arrived_gate.reshape(experts_here, slot_rows).astype(jnp.float32)
    grad_hidden = jnp.einsum("esd,ehd->esh", arrived, w_down, preferred_element_type=jnp.float32)
    gate_pre = pre_acts[:, :, 0].astype(jnp.float32)
    up_pre = pre_acts[:, :, 1].astype(jnp.float32)
    sigmoid_gate = jax.nn.sigmoid(gate_pre)
    activated = gate_pre * sigmoid_gate
    partial_grad = jnp.sum(activated * up_pre * grad_hidden, axis=2)
    scaled = gate_rows[:, :, None] * grad_hidden
    grad_gate = scaled * up_pre * sigmoid_gate * (1.0 + gate_pre * (1.0 - sigmoid_gate))
    grad_up = scaled * activated
    grad_pre = jnp.stack([grad_gate, grad_up], axis=2).astype(jnp.bfloat16)
    partial_grad = partial_grad.reshape(experts_here, peers, capacity)
    summed = lax.psum(partial_grad, "tp")
    returned = lax.all_to_all(summed, "ep", split_axis=1, concat_axis=1, tiled=True)
    grad_gates = returned.reshape(-1)[target_slot]
    return (grad_pre, grad_gates)


def kernel(
    dims,
    x_ref, eid_ref, slot_ref, gate_ref, pre_ref, w_ref,
    out_ref, gg_ref,
    buf, wv, prev, outv, tmp, coef, grad, onehot, meta, mysend, rsend, rrecv,
    own_recv, tp_recv, z_send, x_send, tp_send, loc_sem, w_sem, pre_sem, out_sem,
    m_send, m_recv, r_send, r_recv,
):
    experts, slots, cap, hid, chunks = dims
    m = NX * cap
    mp = onehot.shape[1]
    cbs = hid // 128
    per = 2 * cbs
    unit = m * per
    me = lax.axis_index("ep")
    t = lax.axis_index("tp")
    z, x = me // NX, me % NX
    oz = 1 - x
    last = chunks - 1

    pre_copy = pltpu.make_async_copy(pre_ref, prev, pre_sem)
    pre_copy.start()

    def w_copy(k):
        cols = pl.ds(pl.multiple_of(k * KC, KC), KC)
        return pltpu.make_async_copy(w_ref.at[:, :, cols], wv.at[k], w_sem.at[k])

    def x_src(c):
        return x_ref.at[:, pl.ds(pl.multiple_of(c * KC, KC), KC)]

    def at(zz, xx, h, c):
        return buf.at[zz, h, c, pl.ds(pl.multiple_of(xx * 128, 128), 128), :]

    def loc_copy(c):
        return pltpu.make_async_copy(x_src(c), at(z, x, t, c), loc_sem.at[c])

    @pl.loop(0, chunks)
    def _(c):
        loc_copy(c).start()

    @pl.loop(0, 2 * chunks)
    def _(k):
        w_copy(k).start()

    code = eid_ref[...] * slots + me * cap + slot_ref[...]
    mine = jnp.concatenate(
        [code.astype(jnp.float32), gate_ref[...].astype(jnp.float32)], axis=0
    )
    mysend[...] = mine
    meta[me] = mine

    barrier = pltpu.get_barrier_semaphore()
    n = NZ * NX * 2

    @pl.loop(0, n)
    def _(j):
        @pl.when(j != me * 2 + t)
        def _():
            pl.semaphore_signal(
                barrier, inc=1, device_id={"ep": j // 2, "tp": j % 2}, device_id_type=MESH
            )

    pl.semaphore_wait(barrier, n - 1)

    def m_copy(j):
        return pltpu.make_async_remote_copy(
            src_ref=mysend, dst_ref=meta.at[me], send_sem=m_send.at[j],
            recv_sem=m_recv.at[me], device_id={"ep": j}, device_id_type=MESH,
        )

    @pl.loop(0, NZ * NX)
    def _(j):
        @pl.when(j != me)
        def _():
            m_copy(j).start()

    def along_z(zz, xx, c, up, src=None):
        b = zz * NX + xx
        d = 1 if up else 0
        to = me + NX if up else me - NX
        ref = at(zz, xx, t, c)
        return pltpu.make_async_remote_copy(
            src_ref=ref if src is None else src, dst_ref=ref,
            send_sem=z_send.at[d, b, c], recv_sem=own_recv.at[b, c],
            device_id={"ep": to}, device_id_type=MESH,
        )

    def along_x(zz, c, src=None):
        b = zz * NX + x
        ref = at(zz, x, t, c)
        return pltpu.make_async_remote_copy(
            src_ref=ref if src is None else src, dst_ref=ref,
            send_sem=x_send.at[zz, c], recv_sem=own_recv.at[b, c],
            device_id={"ep": z * NX + oz}, device_id_type=MESH,
        )

    def to_core(zz, xx, c, src=None):
        b = zz * NX + xx
        ref = at(zz, xx, t, c)
        return pltpu.make_async_remote_copy(
            src_ref=ref if src is None else src, dst_ref=ref,
            send_sem=tp_send.at[b, c], recv_sem=tp_recv.at[b, c],
            device_id={"tp": 1 - t}, device_id_type=MESH,
        )

    def arrived(zz, xx, c):
        b = zz * NX + xx
        ref = at(zz, xx, t, c)
        pltpu.make_async_copy(ref, ref, own_recv.at[b, c]).wait()

    def core_arrived(zz, xx, c):
        b = zz * NX + xx
        ref = at(zz, xx, 1 - t, c)
        pltpu.make_async_copy(ref, ref, tp_recv.at[b, c]).wait()

    def order(p):
        inner = jnp.where(p == 0, 1, jnp.where(p == 1, 2, jnp.where(p == 2, 0, 3)))
        low = jnp.where(jnp.logical_or(z == 0, z == NZ - 1), p, inner)
        return jnp.where(z < NZ // 2, low, NZ - 1 - low)

    def chunk(i):
        return lax.rem(i + last, chunks)

    @pl.loop(0, chunks)
    def _(i):
        c = chunk(i)
        along_x(z, c, x_src(c)).start()

        @pl.when(z < NZ - 1)
        def _():
            along_z(z, x, c, True, x_src(c)).start()

        @pl.when(z > 0)
        def _():
            along_z(z, x, c, False, x_src(c)).start()

        to_core(z, x, c, x_src(c)).start()

    pre_copy.wait()

    @pl.loop(0, chunks)
    def _(c):
        loc_copy(c).wait()

    @pl.loop(0, NZ * NX)
    def _(j):
        @pl.when(j != me)
        def _():
            pltpu.make_async_copy(meta.at[j], meta.at[j], m_recv.at[j]).wait()

    @pl.loop(0, 2 * chunks)
    def _(k):
        w_copy(k).wait()

    def from_row(zz, xx, c, up):
        arrived(zz, xx, c)
        if up:
            @pl.when(z < NZ - 1)
            def _():
                along_z(zz, xx, c, True).start()
        else:
            @pl.when(z > 0)
            def _():
                along_z(zz, xx, c, False).start()
        to_core(zz, xx, c).start()

    def r_copy(p, xx, tt):
        return pltpu.make_async_remote_copy(
            src_ref=rsend.at[p, xx], dst_ref=rrecv.at[me * 2 + t],
            send_sem=r_send.at[p, xx, tt], recv_sem=r_recv.at[me * 2 + t],
            device_id={"ep": order(p) * NX + xx, "tp": tt}, device_id_type=MESH,
        )

    def out_copy(p, e):
        rows = pl.ds(pl.multiple_of((e * NZ + order(p)) * unit, unit), unit)
        return pltpu.make_async_copy(outv.at[rows, :], out_ref.at[rows, :], out_sem.at[p, e])

    first_expert = me * experts

    @pl.loop(0, NZ)
    def _(p):
        q = order(p)
        nxt = order(jnp.minimum(p + 1, NZ - 1))
        gates = []
        for e in range(experts):
            rows = pl.ds(pl.multiple_of((e * NZ + q) * unit, unit), unit)
            tmp[...] = prev[rows, :].astype(jnp.float32)
            for cb in range(cbs):
                cols = slice(cb * 128, (cb + 1) * 128)
                a = tmp[pl.ds(cb * 2, m, stride=per), :]
                b = tmp[pl.ds(cb * 2 + 1, m, stride=per), :]
                g = jax.nn.sigmoid(a)
                act = a * g
                coef[e, 0, 0:m, cols] = act * b
                coef[e, 1, 0:m, cols] = b * g * (1.0 + a * (1.0 - g))
                coef[e, 2, 0:m, cols] = act
            base = (first_expert + e) * slots + q * m
            want = (lax.broadcasted_iota(jnp.int32, (mp, 128), 0) + base).astype(jnp.float32)
            gate = jnp.zeros((mp, 1), jnp.float32)
            for xx in range(NX):
                table = meta[q * NX + xx]
                weight = jnp.zeros((mp, 128), jnp.float32)
                hit = jnp.zeros((mp, 128), jnp.float32)
                for k in range(8):
                    same = table[k : k + 1, :] == want
                    hit = jnp.where(same, 1.0, hit)
                    weight = jnp.where(same, table[8 + k : 9 + k, :], weight)
                onehot[e, :, xx * 128 : (xx + 1) * 128] = hit.astype(jnp.bfloat16)
                gate = gate + jnp.sum(weight, axis=1, keepdims=True)
            gates.append(gate)
        grad[...] = jnp.zeros_like(grad)

        @pl.loop(0, chunks)
        def _(i):
            c = chunk(i)

            @pl.when(z - p - 1 >= 0)
            def _():
                from_row(z - p - 1, x, c, True)

                @pl.when(i == last)
                def _():
                    from_row(z - p - 1, oz, last, True)

            @pl.when(z + p + 1 < NZ)
            def _():
                from_row(z + p + 1, x, c, False)

                @pl.when(i == last)
                def _():
                    from_row(z + p + 1, oz, last, False)

            @pl.when(jnp.logical_and(p < NZ - 1, c < last))
            def _():
                along_x(nxt, c).start()

            @pl.when(jnp.logical_or(p == 0, c < last))
            def _():
                arrived(q, oz, c)
                to_core(q, oz, c).start()

            @pl.when(jnp.logical_and(p == 0, c == last))
            def _():
                @pl.when(z < NZ - 1)
                def _():
                    along_z(z, oz, c, True).start()

                @pl.when(z > 0)
                def _():
                    along_z(z, oz, c, False).start()

            core_arrived(q, x, c)
            core_arrived(q, oz, c)
            picks = onehot[...].reshape(experts * mp, NX * 128)
            total = [grad[e] for e in range(experts)]
            for h in range(2):
                rows = jnp.dot(
                    picks, buf[q, h, c], preferred_element_type=jnp.float32
                ).astype(jnp.bfloat16)
                for e in range(experts):
                    total[e] = total[e] + lax.dot_general(
                        rows[e * mp : (e + 1) * mp], wv[h * chunks + c, e],
                        (((1,), (1,)), ((), ())), preferred_element_type=jnp.float32,
                    )
            for e in range(experts):
                grad[e] = total[e]

        sub = lax.broadcasted_iota(jnp.int32, (8, NX * 128), 0)
        back = jnp.zeros((8, NX * 128), jnp.float32)
        for e in range(experts):
            sums = jnp.zeros((m, 1), jnp.float32)
            for cb in range(cbs):
                cols = slice(cb * 128, (cb + 1) * 128)
                gh = grad[e, 0:m, cols]
                sums = sums + jnp.sum(coef[e, 0, 0:m, cols] * gh, axis=1, keepdims=True)
                scaled = gates[e][0:m] * gh
                tmp[pl.ds(cb * 2, m, stride=per), :] = scaled * coef[e, 1, 0:m, cols]
                tmp[pl.ds(cb * 2 + 1, m, stride=per), :] = scaled * coef[e, 2, 0:m, cols]
            picked = onehot[e].astype(jnp.float32)[0:m] * sums
            row = jnp.sum(picked, axis=0, keepdims=True)
            back = jnp.where(sub == e, row, back)
            rows = pl.ds(pl.multiple_of((e * NZ + q) * unit, unit), unit)
            outv[rows, :] = tmp[...].astype(jnp.bfloat16)
            out_copy(p, e).start()
        for xx in range(NX):
            rsend[p, xx] = back[:, xx * 128 : (xx + 1) * 128]
            for tt in range(2):
                own = jnp.logical_and(q * NX + xx == me, t == tt)

                @pl.when(own)
                def _():
                    rrecv[me * 2 + t] = back[:, xx * 128 : (xx + 1) * 128]

                @pl.when(jnp.logical_not(own))
                def _():
                    r_copy(p, xx, tt).start()

    @pl.loop(0, NZ * NX)
    def _(j):
        @pl.when(j != me)
        def _():
            m_copy(j).wait_send()

    @pl.loop(0, chunks)
    def _(i):
        c = chunk(i)
        along_x(z, c).wait_send()

        @pl.when(z < NZ - 1)
        def _():
            along_z(z, x, c, True).wait_send()

        @pl.when(z > 0)
        def _():
            along_z(z, x, c, False).wait_send()

        to_core(z, x, c).wait_send()

    @pl.when(z < NZ - 1)
    def _():
        along_z(z, oz, last, True).wait_send()

    @pl.when(z > 0)
    def _():
        along_z(z, oz, last, False).wait_send()

    def sent_row(zz, xx, c, up):
        if up:
            @pl.when(z < NZ - 1)
            def _():
                along_z(zz, xx, c, True).wait_send()
        else:
            @pl.when(z > 0)
            def _():
                along_z(zz, xx, c, False).wait_send()
        to_core(zz, xx, c).wait_send()

    @pl.loop(0, NZ)
    def _(p):
        q = order(p)
        nxt = order(jnp.minimum(p + 1, NZ - 1))

        @pl.loop(0, chunks)
        def _(i):
            c = chunk(i)

            @pl.when(z - p - 1 >= 0)
            def _():
                sent_row(z - p - 1, x, c, True)

                @pl.when(i == last)
                def _():
                    sent_row(z - p - 1, oz, last, True)

            @pl.when(z + p + 1 < NZ)
            def _():
                sent_row(z + p + 1, x, c, False)

                @pl.when(i == last)
                def _():
                    sent_row(z + p + 1, oz, last, False)

            @pl.when(jnp.logical_and(p < NZ - 1, c < last))
            def _():
                along_x(nxt, c).wait_send()

            @pl.when(jnp.logical_or(p == 0, c < last))
            def _():
                to_core(q, oz, c).wait_send()

        for e in range(experts):
            out_copy(p, e).wait()
        for xx in range(NX):
            for tt in range(2):
                @pl.when(jnp.logical_not(jnp.logical_and(q * NX + xx == me, t == tt)))
                def _():
                    r_copy(p, xx, tt).wait_send()

    @pl.loop(0, n)
    def _(j):
        @pl.when(j != me * 2 + t)
        def _():
            pltpu.make_async_copy(rrecv.at[j], rrecv.at[j], r_recv.at[j]).wait()

    ids = eid_ref[...]
    result = jnp.zeros(ids.shape, jnp.float32)
    for owner in range(NZ * NX):
        both = rrecv[owner * 2] + rrecv[owner * 2 + 1]
        for e in range(experts):
            result = jnp.where(ids == owner * experts + e, both[e : e + 1, :], result)
    gg_ref[...] = result


def relayed(cotangent, gate_weights, expert_ids, slot_ids, pre_acts, w_down):
    experts, slots, _, hid = pre_acts.shape
    peers = lax.axis_size("ep")
    cap = slots // peers
    chunks = cotangent.shape[1] // KC
    chosen = expert_ids.shape[1]
    cbs = hid // 128
    m = NX * cap
    mp = -(-m // 16) * 16
    unit = m * 2 * cbs
    rows = experts * slots * 2 * cbs
    pre = pre_acts.reshape(experts, slots, 2, cbs, 128).transpose(0, 1, 3, 2, 4).reshape(rows, 128)
    vmem = pl.BlockSpec(memory_space=pltpu.VMEM)
    hbm = pl.BlockSpec(memory_space=pl.ANY)
    dma = pltpu.SemaphoreType.DMA
    bf, f32 = jnp.bfloat16, jnp.float32
    out, gg = pl.pallas_call(
        functools.partial(kernel, (experts, slots, cap, hid, chunks)),
        out_shape=(
            jax.ShapeDtypeStruct((rows, 128), bf),
            jax.ShapeDtypeStruct((chosen, 128), f32),
        ),
        in_specs=[hbm, vmem, vmem, vmem, hbm, hbm],
        out_specs=(hbm, vmem),
        scratch_shapes=[
            pltpu.VMEM((NZ, 2, chunks, NX * 128, KC), bf),
            pltpu.VMEM((2 * chunks, experts, hid, KC), bf),
            pltpu.VMEM((rows, 128), bf),
            pltpu.VMEM((rows, 128), bf),
            pltpu.VMEM((unit, 128), f32),
            pltpu.VMEM((experts, 3, mp, hid), f32),
            pltpu.VMEM((experts, mp, hid), f32),
            pltpu.VMEM((experts, mp, NX * 128), bf),
            pltpu.VMEM((peers, 2 * chosen, 128), f32),
            pltpu.VMEM((2 * chosen, 128), f32),
            pltpu.VMEM((NZ, NX, 8, 128), f32),
            pltpu.VMEM((2 * peers, 8, 128), f32),
            dma((peers, chunks)),
            dma((peers, chunks)),
            dma((2, peers, chunks)),
            dma((NZ, chunks)),
            dma((peers, chunks)),
            dma((chunks,)),
            dma((2 * chunks,)),
            dma,
            dma((NZ, experts)),
            dma((peers,)),
            dma((peers,)),
            dma((NZ, NX, 2)),
            dma((2 * peers,)),
        ],
        compiler_params=pltpu.CompilerParams(
            collective_id=0, has_side_effects=True, vmem_limit_bytes=50 * 2**20
        ),
    )(cotangent, expert_ids.T, slot_ids.T, gate_weights.T, pre, w_down)
    grad_pre = (
        out.reshape(experts, slots, cbs, 2, 128)
        .transpose(0, 1, 3, 2, 4)
        .reshape(experts, slots, 2, hid)
    )
    return grad_pre, gg.T


def shards(cotangent, gate_weights, expert_ids, slot_ids, pre_acts, w_down):
    peers = lax.axis_size("ep")
    experts, slots, _, hid = pre_acts.shape
    tokens, chosen = expert_ids.shape
    fits = (
        peers == NZ * NX
        and lax.axis_size("tp") == 2
        and experts * (slots // peers) >= tokens
        and experts <= 8
        and tokens == 128
        and chosen == 8
        and cotangent.shape[1] % KC == 0
        and hid % 128 == 0
    )
    run = relayed if fits else slotted
    return run(cotangent, gate_weights, expert_ids, slot_ids, pre_acts, w_down)


def solution(mesh):
    placed = (
        P(("grp", "ep"), "tp"),
        P(("grp", "ep"), None),
        P(("grp", "ep"), None),
        P(("grp", "ep"), None),
        P("ep", "grp", None, "tp"),
        P("ep", "tp", None),
    )
    return jax.shard_map(
        shards,
        mesh=mesh,
        in_specs=placed,
        out_specs=(P("ep", "grp", None, "tp"), P(("grp", "ep"), None)),
        check_vma=False,
    )
```

```python
import functools

import jax
import jax.numpy as jnp
from jax import lax
from jax.experimental import pallas as pl
from jax.experimental.pallas import tpu as pltpu
from jax.sharding import PartitionSpec as P

MESH = pl.DeviceIdType.MESH
KC = 256
LAG = 2
NZ, NX = 4, 2


def slotted(cotangent, gate_weights, expert_ids, slot_ids, pre_acts, w_down):
    peers = lax.axis_size("ep")
    tok_rows, chosen = expert_ids.shape
    experts_here = w_down.shape[0]
    slot_rows = pre_acts.shape[1]
    capacity = slot_rows // peers
    owners = expert_ids // experts_here
    target_slot = expert_ids % experts_here * slot_rows + owners * capacity + slot_ids
    pair_index = jnp.arange(tok_rows * chosen, dtype=jnp.int32)
    filler = (
        jnp.full((experts_here * slot_rows,), tok_rows * chosen, jnp.int32)
        .at[target_slot.reshape(-1)]
        .set(pair_index)
    )
    padded_gate = jnp.concatenate(
        [gate_weights.reshape(-1), jnp.zeros((1,), gate_weights.dtype)], axis=0
    )
    send_gate = padded_gate[filler].reshape(experts_here, peers, capacity)
    padded = jnp.concatenate(
        [cotangent, jnp.zeros((1, cotangent.shape[1]), cotangent.dtype)], axis=0
    )
    half_rows = lax.all_to_all(
        padded[filler // chosen].reshape(experts_here, peers, capacity, cotangent.shape[1]),
        "ep",
        split_axis=1,
        concat_axis=1,
        tiled=True,
    )
    arrived_gate = lax.all_to_all(send_gate, "ep", split_axis=1, concat_axis=1, tiled=True)
    arrived = lax.all_gather(half_rows, "tp", axis=3, tiled=True)
    arrived = arrived.reshape(experts_here, slot_rows, arrived.shape[3])
    gate_rows = arrived_gate.reshape(experts_here, slot_rows).astype(jnp.float32)
    grad_hidden = jnp.einsum("esd,ehd->esh", arrived, w_down, preferred_element_type=jnp.float32)
    gate_pre = pre_acts[:, :, 0].astype(jnp.float32)
    up_pre = pre_acts[:, :, 1].astype(jnp.float32)
    sigmoid_gate = jax.nn.sigmoid(gate_pre)
    activated = gate_pre * sigmoid_gate
    partial_grad = jnp.sum(activated * up_pre * grad_hidden, axis=2)
    scaled = gate_rows[:, :, None] * grad_hidden
    grad_gate = scaled * up_pre * sigmoid_gate * (1.0 + gate_pre * (1.0 - sigmoid_gate))
    grad_up = scaled * activated
    grad_pre = jnp.stack([grad_gate, grad_up], axis=2).astype(jnp.bfloat16)
    partial_grad = partial_grad.reshape(experts_here, peers, capacity)
    summed = lax.psum(partial_grad, "tp")
    returned = lax.all_to_all(summed, "ep", split_axis=1, concat_axis=1, tiled=True)
    grad_gates = returned.reshape(-1)[target_slot]
    return (grad_pre, grad_gates)


def kernel(
    dims,
    x_ref, eid_hbm, slot_hbm, gate_hbm, pre_ref, w_ref,
    out_ref, gg_ref,
    eid_ref, slot_ref, gate_ref,
    buf, wv, prev, tmp, coef, grad, onehot, gates, meta, mysend, rsend, rrecv,
    own_recv, tp_recv, z_send, x_send, tp_send, loc_sem, w_sem, pre_sem, in_sem,
    m_send, m_recv, r_send, r_recv,
):
    experts, slots, cap, hid, chunks = dims
    m = NX * cap
    mp = onehot.shape[1]
    cbs = hid // 128
    per = 2 * cbs
    unit = m * per
    me = lax.axis_index("ep")
    t = lax.axis_index("tp")
    z, x = me // NX, me % NX
    oz = 1 - x
    last = chunks - 1

    small = [
        pltpu.make_async_copy(src, dst, in_sem.at[i])
        for i, (src, dst) in enumerate(
            [(eid_hbm, eid_ref), (slot_hbm, slot_ref), (gate_hbm, gate_ref)]
        )
    ]
    for copy in small:
        copy.start()
    pre_copy = pltpu.make_async_copy(pre_ref, prev, pre_sem)
    pre_copy.start()

    def w_copy(k):
        cols = pl.ds(pl.multiple_of(k * KC, KC), KC)
        return pltpu.make_async_copy(w_ref.at[:, :, cols], wv.at[k], w_sem.at[k])

    def x_src(c):
        return x_ref.at[:, pl.ds(pl.multiple_of(c * KC, KC), KC)]

    def at(zz, xx, h, c):
        return buf.at[zz, h, c, pl.ds(pl.multiple_of(xx * 128, 128), 128), :]

    def loc_copy(c):
        return pltpu.make_async_copy(x_src(c), at(z, x, t, c), loc_sem.at[c])

    @pl.loop(0, chunks)
    def _(c):
        loc_copy(c).start()

    @pl.loop(0, 2 * chunks)
    def _(k):
        w_copy(k).start()

    barrier = pltpu.get_barrier_semaphore()
    n = NZ * NX * 2

    @pl.loop(0, n)
    def _(j):
        @pl.when(j != me * 2 + t)
        def _():
            pl.semaphore_signal(
                barrier, inc=1, device_id={"ep": j // 2, "tp": j % 2}, device_id_type=MESH
            )

    for copy in small:
        copy.wait()
    code = eid_ref[...] * slots + me * cap + slot_ref[...]
    mine = jnp.concatenate(
        [code.astype(jnp.float32), gate_ref[...].astype(jnp.float32)], axis=0
    )
    mysend[...] = mine
    meta[me] = mine
    pl.semaphore_wait(barrier, n - 1)

    def m_copy(j):
        return pltpu.make_async_remote_copy(
            src_ref=mysend, dst_ref=meta.at[me], send_sem=m_send.at[j],
            recv_sem=m_recv.at[me], device_id={"ep": j}, device_id_type=MESH,
        )

    def along_z(zz, xx, c, up, src=None):
        b = zz * NX + xx
        d = 1 if up else 0
        to = me + NX if up else me - NX
        ref = at(zz, xx, t, c)
        return pltpu.make_async_remote_copy(
            src_ref=ref if src is None else src, dst_ref=ref,
            send_sem=z_send.at[d, b], recv_sem=own_recv.at[b, c],
            device_id={"ep": to}, device_id_type=MESH,
        )

    def along_x(zz, c, src=None):
        b = zz * NX + x
        ref = at(zz, x, t, c)
        return pltpu.make_async_remote_copy(
            src_ref=ref if src is None else src, dst_ref=ref,
            send_sem=x_send.at[zz], recv_sem=own_recv.at[b, c],
            device_id={"ep": z * NX + oz}, device_id_type=MESH,
        )

    def to_core(zz, xx, c, src=None):
        b = zz * NX + xx
        ref = at(zz, xx, t, c)
        return pltpu.make_async_remote_copy(
            src_ref=ref if src is None else src, dst_ref=ref,
            send_sem=tp_send.at[b], recv_sem=tp_recv.at[b, c],
            device_id={"tp": 1 - t}, device_id_type=MESH,
        )

    @pl.loop(0, NZ * NX)
    def _(j):
        @pl.when(j != me)
        def _():
            m_copy(j).start()

    def arrived(zz, xx, c):
        b = zz * NX + xx
        ref = at(zz, xx, t, c)
        pltpu.make_async_copy(ref, ref, own_recv.at[b, c]).wait()

    def core_arrived(zz, xx, c):
        b = zz * NX + xx
        ref = at(zz, xx, 1 - t, c)
        pltpu.make_async_copy(ref, ref, tp_recv.at[b, c]).wait()

    def order(p):
        inner = jnp.where(p == 0, 1, jnp.where(p == 1, 2, jnp.where(p == 2, 0, 3)))
        low = jnp.where(jnp.logical_or(z == 0, z == NZ - 1), p, inner)
        return jnp.where(z < NZ // 2, low, NZ - 1 - low)

    def chunk(i):
        return lax.rem(i + last, chunks)

    @pl.loop(0, chunks)
    def _(i):
        c = chunk(i)
        along_x(z, c, x_src(c)).start()

        @pl.when(z < NZ - 1)
        def _():
            along_z(z, x, c, True, x_src(c)).start()

        @pl.when(z > 0)
        def _():
            along_z(z, x, c, False, x_src(c)).start()

        to_core(z, x, c, x_src(c)).start()

    pre_copy.wait()

    @pl.loop(0, chunks)
    def _(c):
        loc_copy(c).wait()

    @pl.loop(0, NZ * NX)
    def _(j):
        @pl.when(j != me)
        def _():
            pltpu.make_async_copy(meta.at[j], meta.at[j], m_recv.at[j]).wait()

    @pl.loop(0, 2 * chunks)
    def _(k):
        w_copy(k).wait()

    def from_row(zz, xx, c, up):
        arrived(zz, xx, c)
        if up:
            @pl.when(z < NZ - 1)
            def _():
                along_z(zz, xx, c, True).start()
        else:
            @pl.when(z > 0)
            def _():
                along_z(zz, xx, c, False).start()
        to_core(zz, xx, c).start()

    def r_copy(p, xx, tt):
        return pltpu.make_async_remote_copy(
            src_ref=rsend.at[p, xx], dst_ref=rrecv.at[me * 2 + t],
            send_sem=r_send.at[p, xx, tt], recv_sem=r_recv.at[me * 2 + t],
            device_id={"ep": order(p) * NX + xx, "tp": tt}, device_id_type=MESH,
        )

    first_expert = me * experts

    def carry(s):
        p, i = s // chunks, lax.rem(s, chunks)
        c = chunk(i)
        q = order(p)
        nxt = order(jnp.minimum(p + 1, NZ - 1))

        @pl.when(z - p - 1 >= 0)
        def _():
            from_row(z - p - 1, x, c, True)

            @pl.when(i == last)
            def _():
                from_row(z - p - 1, oz, last, True)

        @pl.when(z + p + 1 < NZ)
        def _():
            from_row(z + p + 1, x, c, False)

            @pl.when(i == last)
            def _():
                from_row(z + p + 1, oz, last, False)

        @pl.when(jnp.logical_and(p < NZ - 1, c < last))
        def _():
            along_x(nxt, c).start()

        @pl.when(jnp.logical_or(p == 0, c < last))
        def _():
            arrived(q, oz, c)
            to_core(q, oz, c).start()

        @pl.when(jnp.logical_and(p == 0, c == last))
        def _():
            @pl.when(z < NZ - 1)
            def _():
                along_z(z, oz, c, True).start()

            @pl.when(z > 0)
            def _():
                along_z(z, oz, c, False).start()

    def prepare(p):
        q = order(p)
        for e in range(experts):
            rows = pl.ds(pl.multiple_of((e * NZ + q) * unit, unit), unit)
            tmp[...] = prev[rows, :].astype(jnp.float32)
            for cb in range(cbs):
                cols = slice(cb * 128, (cb + 1) * 128)
                a = tmp[pl.ds(cb * 2, m, stride=per), :]
                b = tmp[pl.ds(cb * 2 + 1, m, stride=per), :]
                g = jax.nn.sigmoid(a)
                act = a * g
                coef[e, 0, 0:m, cols] = act * b
                coef[e, 1, 0:m, cols] = b * g * (1.0 + a * (1.0 - g))
                coef[e, 2, 0:m, cols] = act
            base = (first_expert + e) * slots + q * m
            want = (lax.broadcasted_iota(jnp.int32, (mp, 128), 0) + base).astype(jnp.float32)
            gate = jnp.zeros((mp, 1), jnp.float32)
            for xx in range(NX):
                table = meta[q * NX + xx]
                weight = jnp.zeros((mp, 128), jnp.float32)
                hit = jnp.zeros((mp, 128), jnp.float32)
                for k in range(8):
                    same = table[k : k + 1, :] == want
                    hit = jnp.where(same, 1.0, hit)
                    weight = jnp.where(same, table[8 + k : 9 + k, :], weight)
                onehot[e, :, xx * 128 : (xx + 1) * 128] = hit.astype(jnp.bfloat16)
                gate = gate + jnp.sum(weight, axis=1, keepdims=True)
            gates[e] = jnp.broadcast_to(gate, (mp, 128))
        grad[...] = jnp.zeros_like(grad)

    def multiply(p, c):
        q = order(p)
        core_arrived(q, x, c)
        core_arrived(q, oz, c)
        picks = onehot[...].reshape(experts * mp, NX * 128)
        total = [grad[e] for e in range(experts)]
        for h in range(2):
            rows = jnp.dot(
                picks, buf[q, h, c], preferred_element_type=jnp.float32
            ).astype(jnp.bfloat16)
            for e in range(experts):
                total[e] = total[e] + lax.dot_general(
                    rows[e * mp : (e + 1) * mp], wv[h * chunks + c, e],
                    (((1,), (1,)), ((), ())), preferred_element_type=jnp.float32,
                )
        for e in range(experts):
            grad[e] = total[e]

    def finish(p):
        q = order(p)
        sub = lax.broadcasted_iota(jnp.int32, (8, NX * 128), 0)
        back = jnp.zeros((8, NX * 128), jnp.float32)
        for e in range(experts):
            sums = jnp.zeros((m, 1), jnp.float32)
            for cb in range(cbs):
                cols = slice(cb * 128, (cb + 1) * 128)
                gh = grad[e, 0:m, cols]
                sums = sums + jnp.sum(coef[e, 0, 0:m, cols] * gh, axis=1, keepdims=True)
                scaled = gates[e, 0:m, :] * gh
                tmp[pl.ds(cb * 2, m, stride=per), :] = scaled * coef[e, 1, 0:m, cols]
                tmp[pl.ds(cb * 2 + 1, m, stride=per), :] = scaled * coef[e, 2, 0:m, cols]
            picked = onehot[e].astype(jnp.float32)[0:m] * sums
            row = jnp.sum(picked, axis=0, keepdims=True)
            back = jnp.where(sub == e, row, back)
            rows = pl.ds(pl.multiple_of((e * NZ + q) * unit, unit), unit)
            out_ref[rows, :] = tmp[...].astype(jnp.bfloat16)
        for xx in range(NX):
            rsend[p, xx] = back[:, xx * 128 : (xx + 1) * 128]
            for tt in range(2):
                own = jnp.logical_and(q * NX + xx == me, t == tt)

                @pl.when(own)
                def _():
                    rrecv[me * 2 + t] = back[:, xx * 128 : (xx + 1) * 128]

                @pl.when(jnp.logical_not(own))
                def _():
                    r_copy(p, xx, tt).start()

    @pl.loop(0, NZ * chunks + LAG)
    def _(s):
        @pl.when(s < NZ * chunks)
        def _():
            carry(s)

        @pl.when(s >= LAG)
        def _():
            p, i = (s - LAG) // chunks, lax.rem(s - LAG, chunks)

            @pl.when(i == 0)
            def _():
                prepare(p)

            multiply(p, chunk(i))

            @pl.when(i == last)
            def _():
                finish(p)

    @pl.loop(0, NZ * NX)
    def _(j):
        @pl.when(j != me)
        def _():
            m_copy(j).wait_send()

    def sent(sem, zz, xx, count):
        ref = buf.at[zz, t, 0:count, pl.ds(pl.multiple_of(xx * 128, 128), 128), :]
        pltpu.make_async_copy(ref, ref, sem).wait()

    @pl.loop(0, NZ)
    def _(zz):
        for xx in range(NX):
            sent(tp_send.at[zz * NX + xx], zz, xx, chunks)

        @pl.when(zz == z)
        def _():
            sent(x_send.at[zz], zz, x, chunks)

        @pl.when(zz != z)
        def _():
            sent(x_send.at[zz], zz, x, last)

        @pl.when(jnp.logical_and(zz <= z, z < NZ - 1))
        def _():
            sent(z_send.at[1, zz * NX + x], zz, x, chunks)
            sent(z_send.at[1, zz * NX + oz], zz, oz, 1)

        @pl.when(jnp.logical_and(zz >= z, z > 0))
        def _():
            sent(z_send.at[0, zz * NX + x], zz, x, chunks)
            sent(z_send.at[0, zz * NX + oz], zz, oz, 1)

        for xx in range(NX):
            for tt in range(2):
                @pl.when(jnp.logical_not(jnp.logical_and(order(zz) * NX + xx == me, t == tt)))
                def _():
                    r_copy(zz, xx, tt).wait_send()

    @pl.loop(0, n)
    def _(j):
        @pl.when(j != me * 2 + t)
        def _():
            pltpu.make_async_copy(rrecv.at[j], rrecv.at[j], r_recv.at[j]).wait()

    ids = eid_ref[...]
    result = jnp.zeros(ids.shape, jnp.float32)
    for owner in range(NZ * NX):
        both = rrecv[owner * 2] + rrecv[owner * 2 + 1]
        for e in range(experts):
            result = jnp.where(ids == owner * experts + e, both[e : e + 1, :], result)
    gg_ref[...] = result


def relayed(cotangent, gate_weights, expert_ids, slot_ids, pre_acts, w_down):
    experts, slots, _, hid = pre_acts.shape
    peers = lax.axis_size("ep")
    cap = slots // peers
    chunks = cotangent.shape[1] // KC
    chosen = expert_ids.shape[1]
    cbs = hid // 128
    m = NX * cap
    mp = -(-m // 16) * 16
    unit = m * 2 * cbs
    rows = experts * slots * 2 * cbs
    pre = pre_acts.reshape(experts, slots, 2, cbs, 128).transpose(0, 1, 3, 2, 4).reshape(rows, 128)
    vmem = pl.BlockSpec(memory_space=pltpu.VMEM)
    hbm = pl.BlockSpec(memory_space=pltpu.HBM)
    dma = pltpu.SemaphoreType.DMA
    bf, f32 = jnp.bfloat16, jnp.float32
    out, gg = pl.pallas_call(
        functools.partial(kernel, (experts, slots, cap, hid, chunks)),
        out_shape=(
            jax.ShapeDtypeStruct((rows, 128), bf),
            jax.ShapeDtypeStruct((chosen, 128), f32),
        ),
        in_specs=[hbm] * 6,
        out_specs=(vmem, vmem),
        scratch_shapes=[
            pltpu.VMEM((chosen, 128), jnp.int32),
            pltpu.VMEM((chosen, 128), jnp.int32),
            pltpu.VMEM((chosen, 128), bf),
            pltpu.VMEM((NZ, 2, chunks, NX * 128, KC), bf),
            pltpu.VMEM((2 * chunks, experts, hid, KC), bf),
            pltpu.VMEM((rows, 128), bf),
            pltpu.VMEM((unit, 128), f32),
            pltpu.VMEM((experts, 3, mp, hid), f32),
            pltpu.VMEM((experts, mp, hid), f32),
            pltpu.VMEM((experts, mp, NX * 128), bf),
            pltpu.VMEM((experts, mp, 128), f32),
            pltpu.VMEM((peers, 2 * chosen, 128), f32),
            pltpu.VMEM((2 * chosen, 128), f32),
            pltpu.VMEM((NZ, NX, 8, 128), f32),
            pltpu.VMEM((2 * peers, 8, 128), f32),
            dma((peers, chunks)),
            dma((peers, chunks)),
            dma((2, peers)),
            dma((NZ,)),
            dma((peers,)),
            dma((chunks,)),
            dma((2 * chunks,)),
            dma,
            dma((3,)),
            dma((peers,)),
            dma((peers,)),
            dma((NZ, NX, 2)),
            dma((2 * peers,)),
        ],
        compiler_params=pltpu.CompilerParams(
            collective_id=0, has_side_effects=True, vmem_limit_bytes=50 * 2**20
        ),
    )(cotangent, expert_ids.T, slot_ids.T, gate_weights.T, pre, w_down)
    grad_pre = (
        out.reshape(experts, slots, cbs, 2, 128)
        .transpose(0, 1, 3, 2, 4)
        .reshape(experts, slots, 2, hid)
    )
    return grad_pre, gg.T


def shards(cotangent, gate_weights, expert_ids, slot_ids, pre_acts, w_down):
    peers = lax.axis_size("ep")
    experts, slots, _, hid = pre_acts.shape
    tokens, chosen = expert_ids.shape
    fits = (
        peers == NZ * NX
        and lax.axis_size("tp") == 2
        and experts * (slots // peers) >= tokens
        and experts <= 8
        and tokens == 128
        and chosen == 8
        and cotangent.shape[1] % KC == 0
        and hid % 128 == 0
    )
    run = relayed if fits else slotted
    return run(cotangent, gate_weights, expert_ids, slot_ids, pre_acts, w_down)


def solution(mesh):
    placed = (
        P(("grp", "ep"), "tp"),
        P(("grp", "ep"), None),
        P(("grp", "ep"), None),
        P(("grp", "ep"), None),
        P("ep", "grp", None, "tp"),
        P("ep", "tp", None),
    )
    return jax.shard_map(
        shards,
        mesh=mesh,
        in_specs=placed,
        out_specs=(P("ep", "grp", None, "tp"), P(("grp", "ep"), None)),
        check_vma=False,
    )
```

```python
import functools

import jax
import jax.numpy as jnp
from jax import lax
from jax.experimental import pallas as pl
from jax.experimental.pallas import tpu as pltpu
from jax.sharding import PartitionSpec as P

MESH = pl.DeviceIdType.MESH
KC = 256
LAG = 2
NZ, NX = 4, 2


def slotted(cotangent, gate_weights, expert_ids, slot_ids, pre_acts, w_down):
    peers = lax.axis_size("ep")
    tok_rows, chosen = expert_ids.shape
    experts_here = w_down.shape[0]
    slot_rows = pre_acts.shape[1]
    capacity = slot_rows // peers
    owners = expert_ids // experts_here
    target_slot = expert_ids % experts_here * slot_rows + owners * capacity + slot_ids
    pair_index = jnp.arange(tok_rows * chosen, dtype=jnp.int32)
    filler = (
        jnp.full((experts_here * slot_rows,), tok_rows * chosen, jnp.int32)
        .at[target_slot.reshape(-1)]
        .set(pair_index)
    )
    padded_gate = jnp.concatenate(
        [gate_weights.reshape(-1), jnp.zeros((1,), gate_weights.dtype)], axis=0
    )
    send_gate = padded_gate[filler].reshape(experts_here, peers, capacity)
    padded = jnp.concatenate(
        [cotangent, jnp.zeros((1, cotangent.shape[1]), cotangent.dtype)], axis=0
    )
    half_rows = lax.all_to_all(
        padded[filler // chosen].reshape(experts_here, peers, capacity, cotangent.shape[1]),
        "ep",
        split_axis=1,
        concat_axis=1,
        tiled=True,
    )
    arrived_gate = lax.all_to_all(send_gate, "ep", split_axis=1, concat_axis=1, tiled=True)
    arrived = lax.all_gather(half_rows, "tp", axis=3, tiled=True)
    arrived = arrived.reshape(experts_here, slot_rows, arrived.shape[3])
    gate_rows = arrived_gate.reshape(experts_here, slot_rows).astype(jnp.float32)
    grad_hidden = jnp.einsum("esd,ehd->esh", arrived, w_down, preferred_element_type=jnp.float32)
    gate_pre = pre_acts[:, :, 0].astype(jnp.float32)
    up_pre = pre_acts[:, :, 1].astype(jnp.float32)
    sigmoid_gate = jax.nn.sigmoid(gate_pre)
    activated = gate_pre * sigmoid_gate
    partial_grad = jnp.sum(activated * up_pre * grad_hidden, axis=2)
    scaled = gate_rows[:, :, None] * grad_hidden
    grad_gate = scaled * up_pre * sigmoid_gate * (1.0 + gate_pre * (1.0 - sigmoid_gate))
    grad_up = scaled * activated
    grad_pre = jnp.stack([grad_gate, grad_up], axis=2).astype(jnp.bfloat16)
    partial_grad = partial_grad.reshape(experts_here, peers, capacity)
    summed = lax.psum(partial_grad, "tp")
    returned = lax.all_to_all(summed, "ep", split_axis=1, concat_axis=1, tiled=True)
    grad_gates = returned.reshape(-1)[target_slot]
    return (grad_pre, grad_gates)


def kernel(
    dims,
    x_ref, table_ref, pre_ref, w_ref,
    out_ref, gg_ref,
    buf, wv, prev, tmp, coef, grad, onehot, gates, meta, rsend, rrecv,
    own_recv, tp_recv, z_send, x_send, tp_send, loc_sem, w_sem, pre_sem,
    m_send, m_recv, r_send, r_recv,
):
    experts, slots, cap, hid, chunks = dims
    m = NX * cap
    mp = onehot.shape[1]
    cbs = hid // 128
    per = 2 * cbs
    unit = m * per
    me = lax.axis_index("ep")
    t = lax.axis_index("tp")
    z, x = me // NX, me % NX
    oz = 1 - x
    last = chunks - 1

    pre_copy = pltpu.make_async_copy(pre_ref, prev, pre_sem)
    pre_copy.start()

    def w_copy(k):
        cols = pl.ds(pl.multiple_of(k * KC, KC), KC)
        return pltpu.make_async_copy(w_ref.at[:, :, cols], wv.at[k], w_sem.at[k])

    def x_src(c):
        return x_ref.at[:, pl.ds(pl.multiple_of(c * KC, KC), KC)]

    def at(zz, xx, h, c):
        return buf.at[zz, h, c, pl.ds(pl.multiple_of(xx * 128, 128), 128), :]

    def loc_copy(c):
        return pltpu.make_async_copy(x_src(c), at(z, x, t, c), loc_sem.at[c])

    @pl.loop(0, chunks)
    def _(c):
        loc_copy(c).start()

    @pl.loop(0, 2 * chunks)
    def _(k):
        w_copy(k).start()

    barrier = pltpu.get_barrier_semaphore()
    n = NZ * NX * 2

    @pl.loop(0, n)
    def _(j):
        @pl.when(j != me * 2 + t)
        def _():
            pl.semaphore_signal(
                barrier, inc=1, device_id={"ep": j // 2, "tp": j % 2}, device_id_type=MESH
            )

    meta[me] = table_ref[...]
    pl.semaphore_wait(barrier, n - 1)

    def m_copy(j):
        return pltpu.make_async_remote_copy(
            src_ref=table_ref, dst_ref=meta.at[me], send_sem=m_send.at[j],
            recv_sem=m_recv.at[me], device_id={"ep": j}, device_id_type=MESH,
        )

    def along_z(zz, xx, c, up, src=None):
        b = zz * NX + xx
        d = 1 if up else 0
        to = me + NX if up else me - NX
        ref = at(zz, xx, t, c)
        return pltpu.make_async_remote_copy(
            src_ref=ref if src is None else src, dst_ref=ref,
            send_sem=z_send.at[d, b], recv_sem=own_recv.at[b, c],
            device_id={"ep": to}, device_id_type=MESH,
        )

    def along_x(zz, c, src=None):
        b = zz * NX + x
        ref = at(zz, x, t, c)
        return pltpu.make_async_remote_copy(
            src_ref=ref if src is None else src, dst_ref=ref,
            send_sem=x_send.at[zz], recv_sem=own_recv.at[b, c],
            device_id={"ep": z * NX + oz}, device_id_type=MESH,
        )

    def to_core(zz, xx, c, src=None):
        b = zz * NX + xx
        ref = at(zz, xx, t, c)
        return pltpu.make_async_remote_copy(
            src_ref=ref if src is None else src, dst_ref=ref,
            send_sem=tp_send.at[b], recv_sem=tp_recv.at[b, c],
            device_id={"tp": 1 - t}, device_id_type=MESH,
        )

    def arrived(zz, xx, c):
        b = zz * NX + xx
        ref = at(zz, xx, t, c)
        pltpu.make_async_copy(ref, ref, own_recv.at[b, c]).wait()

    def core_arrived(zz, xx, c):
        b = zz * NX + xx
        ref = at(zz, xx, 1 - t, c)
        pltpu.make_async_copy(ref, ref, tp_recv.at[b, c]).wait()

    def order(p):
        inner = jnp.where(p == 0, 1, jnp.where(p == 1, 2, jnp.where(p == 2, 0, 3)))
        low = jnp.where(jnp.logical_or(z == 0, z == NZ - 1), p, inner)
        return jnp.where(z < NZ // 2, low, NZ - 1 - low)

    def chunk(i):
        return lax.rem(i + last, chunks)

    @pl.loop(0, chunks)
    def _(i):
        c = chunk(i)
        along_x(z, c, x_src(c)).start()

        @pl.when(z < NZ - 1)
        def _():
            along_z(z, x, c, True, x_src(c)).start()

        @pl.when(z > 0)
        def _():
            along_z(z, x, c, False, x_src(c)).start()

        to_core(z, x, c, x_src(c)).start()

    @pl.loop(0, NZ * NX)
    def _(j):
        @pl.when(j != me)
        def _():
            m_copy(j).start()

    def from_row(zz, xx, c, up):
        arrived(zz, xx, c)
        if up:
            @pl.when(z < NZ - 1)
            def _():
                along_z(zz, xx, c, True).start()
        else:
            @pl.when(z > 0)
            def _():
                along_z(zz, xx, c, False).start()
        to_core(zz, xx, c).start()

    def r_copy(p, xx, tt):
        return pltpu.make_async_remote_copy(
            src_ref=rsend.at[p, xx], dst_ref=rrecv.at[me * 2 + t],
            send_sem=r_send.at[p, xx, tt], recv_sem=r_recv.at[me * 2 + t],
            device_id={"ep": order(p) * NX + xx, "tp": tt}, device_id_type=MESH,
        )

    first_expert = me * experts

    def carry(s):
        p, i = s // chunks, lax.rem(s, chunks)
        c = chunk(i)
        q = order(p)
        nxt = order(jnp.minimum(p + 1, NZ - 1))

        @pl.when(z - p - 1 >= 0)
        def _():
            from_row(z - p - 1, x, c, True)

            @pl.when(i == last)
            def _():
                from_row(z - p - 1, oz, last, True)

        @pl.when(z + p + 1 < NZ)
        def _():
            from_row(z + p + 1, x, c, False)

            @pl.when(i == last)
            def _():
                from_row(z + p + 1, oz, last, False)

        @pl.when(jnp.logical_and(p < NZ - 1, c < last))
        def _():
            along_x(nxt, c).start()

        @pl.when(jnp.logical_or(p == 0, c < last))
        def _():
            arrived(q, oz, c)
            to_core(q, oz, c).start()

        @pl.when(jnp.logical_and(p == 0, c == last))
        def _():
            @pl.when(z < NZ - 1)
            def _():
                along_z(z, oz, c, True).start()

            @pl.when(z > 0)
            def _():
                along_z(z, oz, c, False).start()

    def prepare(p):
        q = order(p)
        for e in range(experts):
            rows = pl.ds(pl.multiple_of((e * NZ + q) * unit, unit), unit)
            tmp[...] = prev[rows, :].astype(jnp.float32)
            for cb in range(cbs):
                cols = slice(cb * 128, (cb + 1) * 128)
                a = tmp[pl.ds(cb * 2, m, stride=per), :]
                b = tmp[pl.ds(cb * 2 + 1, m, stride=per), :]
                g = jax.nn.sigmoid(a)
                act = a * g
                coef[e, 0, 0:m, cols] = act * b
                coef[e, 1, 0:m, cols] = b * g * (1.0 + a * (1.0 - g))
                coef[e, 2, 0:m, cols] = act
            base = (first_expert + e) * slots + q * m
            want = (lax.broadcasted_iota(jnp.int32, (mp, 128), 0) + base).astype(jnp.float32)
            gate = jnp.zeros((mp, 1), jnp.float32)
            for xx in range(NX):
                table = meta[q * NX + xx]
                weight = jnp.zeros((mp, 128), jnp.float32)
                hit = jnp.zeros((mp, 128), jnp.float32)
                for k in range(8):
                    same = table[k : k + 1, :] == want
                    hit = jnp.where(same, 1.0, hit)
                    weight = jnp.where(same, table[8 + k : 9 + k, :], weight)
                onehot[e, :, xx * 128 : (xx + 1) * 128] = hit.astype(jnp.bfloat16)
                gate = gate + jnp.sum(weight, axis=1, keepdims=True)
            gates[e] = jnp.broadcast_to(gate, (mp, 128))
        grad[...] = jnp.zeros_like(grad)

    def multiply(p, c):
        q = order(p)
        core_arrived(q, x, c)
        core_arrived(q, oz, c)
        picks = onehot[...].reshape(experts * mp, NX * 128)
        total = [grad[e] for e in range(experts)]
        for h in range(2):
            rows = jnp.dot(
                picks, buf[q, h, c], preferred_element_type=jnp.float32
            ).astype(jnp.bfloat16)
            for e in range(experts):
                total[e] = total[e] + lax.dot_general(
                    rows[e * mp : (e + 1) * mp], wv[h * chunks + c, e],
                    (((1,), (1,)), ((), ())), preferred_element_type=jnp.float32,
                )
        for e in range(experts):
            grad[e] = total[e]

    def finish(p):
        q = order(p)
        sub = lax.broadcasted_iota(jnp.int32, (8, NX * 128), 0)
        back = jnp.zeros((8, NX * 128), jnp.float32)
        for e in range(experts):
            sums = jnp.zeros((m, 1), jnp.float32)
            for cb in range(cbs):
                cols = slice(cb * 128, (cb + 1) * 128)
                gh = grad[e, 0:m, cols]
                sums = sums + jnp.sum(coef[e, 0, 0:m, cols] * gh, axis=1, keepdims=True)
                scaled = gates[e, 0:m, :] * gh
                tmp[pl.ds(cb * 2, m, stride=per), :] = scaled * coef[e, 1, 0:m, cols]
                tmp[pl.ds(cb * 2 + 1, m, stride=per), :] = scaled * coef[e, 2, 0:m, cols]
            picked = onehot[e].astype(jnp.float32)[0:m] * sums
            row = jnp.sum(picked, axis=0, keepdims=True)
            back = jnp.where(sub == e, row, back)
            rows = pl.ds(pl.multiple_of((e * NZ + q) * unit, unit), unit)
            out_ref[rows, :] = tmp[...].astype(jnp.bfloat16)
        for xx in range(NX):
            rsend[p, xx] = back[:, xx * 128 : (xx + 1) * 128]
            for tt in range(2):
                own = jnp.logical_and(q * NX + xx == me, t == tt)

                @pl.when(own)
                def _():
                    rrecv[me * 2 + t] = back[:, xx * 128 : (xx + 1) * 128]

                @pl.when(jnp.logical_not(own))
                def _():
                    r_copy(p, xx, tt).start()

    @pl.loop(0, NZ * chunks + LAG)
    def _(s):
        @pl.when(s < NZ * chunks)
        def _():
            carry(s)

        @pl.when(s >= LAG)
        def _():
            p, i = (s - LAG) // chunks, lax.rem(s - LAG, chunks)

            @pl.when(s == LAG)
            def _():
                pre_copy.wait()

                @pl.loop(0, chunks)
                def _(c):
                    loc_copy(c).wait()

                @pl.loop(0, NZ * NX)
                def _(j):
                    @pl.when(j != me)
                    def _():
                        pltpu.make_async_copy(meta.at[j], meta.at[j], m_recv.at[j]).wait()

                @pl.loop(0, 2 * chunks)
                def _(k):
                    w_copy(k).wait()

            @pl.when(i == 0)
            def _():
                prepare(p)

            multiply(p, chunk(i))

            @pl.when(i == last)
            def _():
                finish(p)

    @pl.loop(0, NZ * NX)
    def _(j):
        @pl.when(j != me)
        def _():
            m_copy(j).wait_send()

    def sent(sem, zz, xx, count):
        ref = buf.at[zz, t, 0:count, pl.ds(pl.multiple_of(xx * 128, 128), 128), :]
        pltpu.make_async_copy(ref, ref, sem).wait()

    @pl.loop(0, NZ)
    def _(zz):
        for xx in range(NX):
            sent(tp_send.at[zz * NX + xx], zz, xx, chunks)

        @pl.when(zz == z)
        def _():
            sent(x_send.at[zz], zz, x, chunks)

        @pl.when(zz != z)
        def _():
            sent(x_send.at[zz], zz, x, last)

        @pl.when(jnp.logical_and(zz <= z, z < NZ - 1))
        def _():
            sent(z_send.at[1, zz * NX + x], zz, x, chunks)
            sent(z_send.at[1, zz * NX + oz], zz, oz, 1)

        @pl.when(jnp.logical_and(zz >= z, z > 0))
        def _():
            sent(z_send.at[0, zz * NX + x], zz, x, chunks)
            sent(z_send.at[0, zz * NX + oz], zz, oz, 1)

        for xx in range(NX):
            for tt in range(2):
                @pl.when(jnp.logical_not(jnp.logical_and(order(zz) * NX + xx == me, t == tt)))
                def _():
                    r_copy(zz, xx, tt).wait_send()

    @pl.loop(0, n)
    def _(j):
        @pl.when(j != me * 2 + t)
        def _():
            pltpu.make_async_copy(rrecv.at[j], rrecv.at[j], r_recv.at[j]).wait()

    code = table_ref[0:8, :]
    result = jnp.zeros(code.shape, jnp.float32)
    for owner in range(NZ * NX):
        both = rrecv[owner * 2] + rrecv[owner * 2 + 1]
        for e in range(experts):
            start = float((owner * experts + e) * slots)
            here = jnp.logical_and(code >= start, code < start + slots)
            result = jnp.where(here, both[e : e + 1, :], result)
    gg_ref[...] = result


def relayed(cotangent, gate_weights, expert_ids, slot_ids, pre_acts, w_down):
    experts, slots, _, hid = pre_acts.shape
    peers = lax.axis_size("ep")
    cap = slots // peers
    chunks = cotangent.shape[1] // KC
    chosen = expert_ids.shape[1]
    cbs = hid // 128
    m = NX * cap
    mp = -(-m // 16) * 16
    unit = m * 2 * cbs
    rows = experts * slots * 2 * cbs
    pre = pre_acts.reshape(experts, slots, 2, cbs, 128).transpose(0, 1, 3, 2, 4).reshape(rows, 128)
    code = expert_ids * slots + lax.axis_index("ep") * cap + slot_ids
    table = jnp.concatenate([code.T.astype(jnp.float32), gate_weights.T.astype(jnp.float32)])
    vmem = pl.BlockSpec(memory_space=pltpu.VMEM)
    hbm = pl.BlockSpec(memory_space=pltpu.HBM)
    dma = pltpu.SemaphoreType.DMA
    bf, f32 = jnp.bfloat16, jnp.float32
    out, gg = pl.pallas_call(
        functools.partial(kernel, (experts, slots, cap, hid, chunks)),
        out_shape=(
            jax.ShapeDtypeStruct((rows, 128), bf),
            jax.ShapeDtypeStruct((chosen, 128), f32),
        ),
        in_specs=[hbm, vmem, hbm, hbm],
        out_specs=(vmem, vmem),
        scratch_shapes=[
            pltpu.VMEM((NZ, 2, chunks, NX * 128, KC), bf),
            pltpu.VMEM((2 * chunks, experts, hid, KC), bf),
            pltpu.VMEM((rows, 128), bf),
            pltpu.VMEM((unit, 128), f32),
            pltpu.VMEM((experts, 3, mp, hid), f32),
            pltpu.VMEM((experts, mp, hid), f32),
            pltpu.VMEM((experts, mp, NX * 128), bf),
            pltpu.VMEM((experts, mp, 128), f32),
            pltpu.VMEM((peers, 2 * chosen, 128), f32),
            pltpu.VMEM((NZ, NX, 8, 128), f32),
            pltpu.VMEM((2 * peers, 8, 128), f32),
            dma((peers, chunks)),
            dma((peers, chunks)),
            dma((2, peers)),
            dma((NZ,)),
            dma((peers,)),
            dma((chunks,)),
            dma((2 * chunks,)),
            dma,
            dma((peers,)),
            dma((peers,)),
            dma((NZ, NX, 2)),
            dma((2 * peers,)),
        ],
        compiler_params=pltpu.CompilerParams(
            collective_id=0, has_side_effects=True, vmem_limit_bytes=50 * 2**20
        ),
    )(cotangent, table, pre, w_down)
    grad_pre = (
        out.reshape(experts, slots, cbs, 2, 128)
        .transpose(0, 1, 3, 2, 4)
        .reshape(experts, slots, 2, hid)
    )
    return grad_pre, gg.T


def shards(cotangent, gate_weights, expert_ids, slot_ids, pre_acts, w_down):
    peers = lax.axis_size("ep")
    experts, slots, _, hid = pre_acts.shape
    tokens, chosen = expert_ids.shape
    fits = (
        peers == NZ * NX
        and lax.axis_size("tp") == 2
        and experts * (slots // peers) >= tokens
        and experts <= 8
        and tokens == 128
        and chosen == 8
        and cotangent.shape[1] % KC == 0
        and hid % 128 == 0
    )
    run = relayed if fits else slotted
    return run(cotangent, gate_weights, expert_ids, slot_ids, pre_acts, w_down)


def solution(mesh):
    placed = (
        P(("grp", "ep"), "tp"),
        P(("grp", "ep"), None),
        P(("grp", "ep"), None),
        P(("grp", "ep"), None),
        P("ep", "grp", None, "tp"),
        P("ep", "tp", None),
    )
    return jax.shard_map(
        shards,
        mesh=mesh,
        in_specs=placed,
        out_specs=(P("ep", "grp", None, "tp"), P(("grp", "ep"), None)),
        check_vma=False,
    )
```

```python
import functools

import jax
import jax.numpy as jnp
from jax import lax
from jax.experimental import pallas as pl
from jax.experimental.pallas import tpu as pltpu
from jax.sharding import PartitionSpec as P

MESH = pl.DeviceIdType.MESH
KC = 256
LAG = 1
NZ, NX = 4, 2


def slotted(cotangent, gate_weights, expert_ids, slot_ids, pre_acts, w_down):
    peers = lax.axis_size("ep")
    tok_rows, chosen = expert_ids.shape
    experts_here = w_down.shape[0]
    slot_rows = pre_acts.shape[1]
    capacity = slot_rows // peers
    owners = expert_ids // experts_here
    target_slot = expert_ids % experts_here * slot_rows + owners * capacity + slot_ids
    pair_index = jnp.arange(tok_rows * chosen, dtype=jnp.int32)
    filler = (
        jnp.full((experts_here * slot_rows,), tok_rows * chosen, jnp.int32)
        .at[target_slot.reshape(-1)]
        .set(pair_index)
    )
    padded_gate = jnp.concatenate(
        [gate_weights.reshape(-1), jnp.zeros((1,), gate_weights.dtype)], axis=0
    )
    send_gate = padded_gate[filler].reshape(experts_here, peers, capacity)
    padded = jnp.concatenate(
        [cotangent, jnp.zeros((1, cotangent.shape[1]), cotangent.dtype)], axis=0
    )
    half_rows = lax.all_to_all(
        padded[filler // chosen].reshape(experts_here, peers, capacity, cotangent.shape[1]),
        "ep",
        split_axis=1,
        concat_axis=1,
        tiled=True,
    )
    arrived_gate = lax.all_to_all(send_gate, "ep", split_axis=1, concat_axis=1, tiled=True)
    arrived = lax.all_gather(half_rows, "tp", axis=3, tiled=True)
    arrived = arrived.reshape(experts_here, slot_rows, arrived.shape[3])
    gate_rows = arrived_gate.reshape(experts_here, slot_rows).astype(jnp.float32)
    grad_hidden = jnp.einsum("esd,ehd->esh", arrived, w_down, preferred_element_type=jnp.float32)
    gate_pre = pre_acts[:, :, 0].astype(jnp.float32)
    up_pre = pre_acts[:, :, 1].astype(jnp.float32)
    sigmoid_gate = jax.nn.sigmoid(gate_pre)
    activated = gate_pre * sigmoid_gate
    partial_grad = jnp.sum(activated * up_pre * grad_hidden, axis=2)
    scaled = gate_rows[:, :, None] * grad_hidden
    grad_gate = scaled * up_pre * sigmoid_gate * (1.0 + gate_pre * (1.0 - sigmoid_gate))
    grad_up = scaled * activated
    grad_pre = jnp.stack([grad_gate, grad_up], axis=2).astype(jnp.bfloat16)
    partial_grad = partial_grad.reshape(experts_here, peers, capacity)
    summed = lax.psum(partial_grad, "tp")
    returned = lax.all_to_all(summed, "ep", split_axis=1, concat_axis=1, tiled=True)
    grad_gates = returned.reshape(-1)[target_slot]
    return (grad_pre, grad_gates)


def kernel(
    dims,
    x_ref, table_ref, pre_ref, w_ref,
    out_ref, gg_ref,
    buf, wv, prev, tmp, coef, grad, onehot, gates, meta, rsend, rrecv,
    own_recv, tp_recv, z_send, x_send, tp_send, loc_sem, w_sem, pre_sem,
    m_send, m_recv, r_send, r_recv,
):
    experts, slots, cap, hid, chunks = dims
    m = NX * cap
    mp = onehot.shape[1]
    cbs = hid // 128
    per = 2 * cbs
    unit = m * per
    me = lax.axis_index("ep")
    t = lax.axis_index("tp")
    z, x = me // NX, me % NX
    oz = 1 - x
    last = chunks - 1

    pre_copy = pltpu.make_async_copy(pre_ref, prev, pre_sem)
    pre_copy.start()

    def w_copy(k):
        cols = pl.ds(pl.multiple_of(k * KC, KC), KC)
        return pltpu.make_async_copy(w_ref.at[:, :, cols], wv.at[k], w_sem.at[k])

    def x_src(c):
        return x_ref.at[:, pl.ds(pl.multiple_of(c * KC, KC), KC)]

    def at(zz, xx, h, c):
        return buf.at[zz, h, c, pl.ds(pl.multiple_of(xx * 128, 128), 128), :]

    def loc_copy(c):
        return pltpu.make_async_copy(x_src(c), at(z, x, t, c), loc_sem.at[c])

    @pl.loop(0, chunks)
    def _(c):
        loc_copy(c).start()

    @pl.loop(0, 2 * chunks)
    def _(k):
        w_copy(k).start()

    barrier = pltpu.get_barrier_semaphore()
    n = NZ * NX * 2

    @pl.loop(0, n)
    def _(j):
        @pl.when(j != me * 2 + t)
        def _():
            pl.semaphore_signal(
                barrier, inc=1, device_id={"ep": j // 2, "tp": j % 2}, device_id_type=MESH
            )

    meta[me] = table_ref[...]
    pl.semaphore_wait(barrier, n - 1)

    def m_copy(j):
        return pltpu.make_async_remote_copy(
            src_ref=table_ref, dst_ref=meta.at[me], send_sem=m_send.at[j],
            recv_sem=m_recv.at[me], device_id={"ep": j}, device_id_type=MESH,
        )

    def along_z(zz, xx, c, up, src=None):
        b = zz * NX + xx
        d = 1 if up else 0
        to = me + NX if up else me - NX
        ref = at(zz, xx, t, c)
        return pltpu.make_async_remote_copy(
            src_ref=ref if src is None else src, dst_ref=ref,
            send_sem=z_send.at[d, b], recv_sem=own_recv.at[b, c],
            device_id={"ep": to}, device_id_type=MESH,
        )

    def along_x(zz, c, src=None):
        b = zz * NX + x
        ref = at(zz, x, t, c)
        return pltpu.make_async_remote_copy(
            src_ref=ref if src is None else src, dst_ref=ref,
            send_sem=x_send.at[zz], recv_sem=own_recv.at[b, c],
            device_id={"ep": z * NX + oz}, device_id_type=MESH,
        )

    def to_core(zz, xx, c, src=None):
        b = zz * NX + xx
        ref = at(zz, xx, t, c)
        return pltpu.make_async_remote_copy(
            src_ref=ref if src is None else src, dst_ref=ref,
            send_sem=tp_send.at[b], recv_sem=tp_recv.at[b, c],
            device_id={"tp": 1 - t}, device_id_type=MESH,
        )

    def arrived(zz, xx, c):
        b = zz * NX + xx
        ref = at(zz, xx, t, c)
        pltpu.make_async_copy(ref, ref, own_recv.at[b, c]).wait()

    def core_arrived(zz, xx, c):
        b = zz * NX + xx
        ref = at(zz, xx, 1 - t, c)
        pltpu.make_async_copy(ref, ref, tp_recv.at[b, c]).wait()

    def order(p):
        inner = jnp.where(p == 0, 1, jnp.where(p == 1, 2, jnp.where(p == 2, 0, 3)))
        low = jnp.where(jnp.logical_or(z == 0, z == NZ - 1), p, inner)
        return jnp.where(z < NZ // 2, low, NZ - 1 - low)

    def chunk(i):
        return lax.rem(i + last, chunks)

    @pl.loop(0, chunks)
    def _(i):
        c = chunk(i)
        along_x(z, c, x_src(c)).start()

        @pl.when(z < NZ - 1)
        def _():
            along_z(z, x, c, True, x_src(c)).start()

        @pl.when(z > 0)
        def _():
            along_z(z, x, c, False, x_src(c)).start()

        to_core(z, x, c, x_src(c)).start()

    @pl.loop(0, NZ * NX)
    def _(j):
        @pl.when(j != me)
        def _():
            m_copy(j).start()

    def from_row(zz, xx, c, up):
        arrived(zz, xx, c)
        if up:
            @pl.when(z < NZ - 1)
            def _():
                along_z(zz, xx, c, True).start()
        else:
            @pl.when(z > 0)
            def _():
                along_z(zz, xx, c, False).start()
        to_core(zz, xx, c).start()

    def r_copy(p, xx, tt):
        return pltpu.make_async_remote_copy(
            src_ref=rsend.at[p, xx], dst_ref=rrecv.at[me * 2 + t],
            send_sem=r_send.at[p, xx, tt], recv_sem=r_recv.at[me * 2 + t],
            device_id={"ep": order(p) * NX + xx, "tp": tt}, device_id_type=MESH,
        )

    first_expert = me * experts

    def carry(s):
        p, i = s // chunks, lax.rem(s, chunks)
        c = chunk(i)
        q = order(p)
        nxt = order(jnp.minimum(p + 1, NZ - 1))

        @pl.when(z - p - 1 >= 0)
        def _():
            from_row(z - p - 1, x, c, True)

            @pl.when(i == last)
            def _():
                from_row(z - p - 1, oz, last, True)

        @pl.when(z + p + 1 < NZ)
        def _():
            from_row(z + p + 1, x, c, False)

            @pl.when(i == last)
            def _():
                from_row(z + p + 1, oz, last, False)

        @pl.when(jnp.logical_and(p < NZ - 1, c < last))
        def _():
            along_x(nxt, c).start()

        @pl.when(jnp.logical_or(p == 0, c < last))
        def _():
            arrived(q, oz, c)
            to_core(q, oz, c).start()

        @pl.when(jnp.logical_and(p == 0, c == last))
        def _():
            @pl.when(z < NZ - 1)
            def _():
                along_z(z, oz, c, True).start()

            @pl.when(z > 0)
            def _():
                along_z(z, oz, c, False).start()

    def prepare(p):
        q = order(p)
        for e in range(experts):
            rows = pl.ds(pl.multiple_of((e * NZ + q) * unit, unit), unit)
            tmp[...] = prev[rows, :].astype(jnp.float32)
            for cb in range(cbs):
                cols = slice(cb * 128, (cb + 1) * 128)
                a = tmp[pl.ds(cb * 2, m, stride=per), :]
                b = tmp[pl.ds(cb * 2 + 1, m, stride=per), :]
                g = jax.nn.sigmoid(a)
                act = a * g
                coef[e, 0, 0:m, cols] = act * b
                coef[e, 1, 0:m, cols] = b * g * (1.0 + a * (1.0 - g))
                coef[e, 2, 0:m, cols] = act
            base = (first_expert + e) * slots + q * m
            want = (lax.broadcasted_iota(jnp.int32, (mp, 128), 0) + base).astype(jnp.float32)
            gate = jnp.zeros((mp, 1), jnp.float32)
            for xx in range(NX):
                table = meta[q * NX + xx]
                weight = jnp.zeros((mp, 128), jnp.float32)
                hit = jnp.zeros((mp, 128), jnp.float32)
                for k in range(8):
                    same = table[k : k + 1, :] == want
                    hit = jnp.where(same, 1.0, hit)
                    weight = jnp.where(same, table[8 + k : 9 + k, :], weight)
                onehot[e, :, xx * 128 : (xx + 1) * 128] = hit.astype(jnp.bfloat16)
                gate = gate + jnp.sum(weight, axis=1, keepdims=True)
            gates[e] = jnp.broadcast_to(gate, (mp, 128))
        grad[...] = jnp.zeros_like(grad)

    def multiply(p, c):
        q = order(p)
        core_arrived(q, x, c)
        core_arrived(q, oz, c)
        picks = onehot[...].reshape(experts * mp, NX * 128)
        total = [grad[e] for e in range(experts)]
        for h in range(2):
            rows = jnp.dot(
                picks, buf[q, h, c], preferred_element_type=jnp.float32
            ).astype(jnp.bfloat16)
            for e in range(experts):
                total[e] = total[e] + lax.dot_general(
                    rows[e * mp : (e + 1) * mp], wv[h * chunks + c, e],
                    (((1,), (1,)), ((), ())), preferred_element_type=jnp.float32,
                )
        for e in range(experts):
            grad[e] = total[e]

    def finish(p):
        q = order(p)
        sub = lax.broadcasted_iota(jnp.int32, (8, NX * 128), 0)
        back = jnp.zeros((8, NX * 128), jnp.float32)
        for e in range(experts):
            sums = jnp.zeros((m, 1), jnp.float32)
            for cb in range(cbs):
                cols = slice(cb * 128, (cb + 1) * 128)
                gh = grad[e, 0:m, cols]
                sums = sums + jnp.sum(coef[e, 0, 0:m, cols] * gh, axis=1, keepdims=True)
                scaled = gates[e, 0:m, :] * gh
                tmp[pl.ds(cb * 2, m, stride=per), :] = scaled * coef[e, 1, 0:m, cols]
                tmp[pl.ds(cb * 2 + 1, m, stride=per), :] = scaled * coef[e, 2, 0:m, cols]
            picked = onehot[e].astype(jnp.float32)[0:m] * sums
            row = jnp.sum(picked, axis=0, keepdims=True)
            back = jnp.where(sub == e, row, back)
            rows = pl.ds(pl.multiple_of((e * NZ + q) * unit, unit), unit)
            out_ref[rows, :] = tmp[...].astype(jnp.bfloat16)
        for xx in range(NX):
            rsend[p, xx] = back[:, xx * 128 : (xx + 1) * 128]
            for tt in range(2):
                own = jnp.logical_and(q * NX + xx == me, t == tt)

                @pl.when(own)
                def _():
                    rrecv[me * 2 + t] = back[:, xx * 128 : (xx + 1) * 128]

                @pl.when(jnp.logical_not(own))
                def _():
                    r_copy(p, xx, tt).start()

    @pl.loop(0, NZ * chunks + LAG)
    def _(s):
        @pl.when(s < NZ * chunks)
        def _():
            carry(s)

        @pl.when(s >= LAG)
        def _():
            p, i = (s - LAG) // chunks, lax.rem(s - LAG, chunks)

            @pl.when(s == LAG)
            def _():
                pre_copy.wait()

                @pl.loop(0, chunks)
                def _(c):
                    loc_copy(c).wait()

                @pl.loop(0, NZ * NX)
                def _(j):
                    @pl.when(j != me)
                    def _():
                        pltpu.make_async_copy(meta.at[j], meta.at[j], m_recv.at[j]).wait()

                @pl.loop(0, 2 * chunks)
                def _(k):
                    w_copy(k).wait()

            @pl.when(i == 0)
            def _():
                prepare(p)

            multiply(p, chunk(i))

            @pl.when(i == last)
            def _():
                finish(p)

    @pl.loop(0, NZ * NX)
    def _(j):
        @pl.when(j != me)
        def _():
            m_copy(j).wait_send()

    def sent(sem, zz, xx, count):
        ref = buf.at[zz, t, 0:count, pl.ds(pl.multiple_of(xx * 128, 128), 128), :]
        pltpu.make_async_copy(ref, ref, sem).wait()

    @pl.loop(0, NZ)
    def _(zz):
        for xx in range(NX):
            sent(tp_send.at[zz * NX + xx], zz, xx, chunks)

        @pl.when(zz == z)
        def _():
            sent(x_send.at[zz], zz, x, chunks)

        @pl.when(zz != z)
        def _():
            sent(x_send.at[zz], zz, x, last)

        @pl.when(jnp.logical_and(zz <= z, z < NZ - 1))
        def _():
            sent(z_send.at[1, zz * NX + x], zz, x, chunks)
            sent(z_send.at[1, zz * NX + oz], zz, oz, 1)

        @pl.when(jnp.logical_and(zz >= z, z > 0))
        def _():
            sent(z_send.at[0, zz * NX + x], zz, x, chunks)
            sent(z_send.at[0, zz * NX + oz], zz, oz, 1)

        for xx in range(NX):
            for tt in range(2):
                @pl.when(jnp.logical_not(jnp.logical_and(order(zz) * NX + xx == me, t == tt)))
                def _():
                    r_copy(zz, xx, tt).wait_send()

    @pl.loop(0, n)
    def _(j):
        @pl.when(j != me * 2 + t)
        def _():
            pltpu.make_async_copy(rrecv.at[j], rrecv.at[j], r_recv.at[j]).wait()

    code = table_ref[0:8, :]
    result = jnp.zeros(code.shape, jnp.float32)
    for owner in range(NZ * NX):
        both = rrecv[owner * 2] + rrecv[owner * 2 + 1]
        for e in range(experts):
            start = float((owner * experts + e) * slots)
            here = jnp.logical_and(code >= start, code < start + slots)
            result = jnp.where(here, both[e : e + 1, :], result)
    gg_ref[...] = result


def relayed(cotangent, gate_weights, expert_ids, slot_ids, pre_acts, w_down):
    experts, slots, _, hid = pre_acts.shape
    peers = lax.axis_size("ep")
    cap = slots // peers
    chunks = cotangent.shape[1] // KC
    chosen = expert_ids.shape[1]
    cbs = hid // 128
    m = NX * cap
    mp = -(-m // 16) * 16
    unit = m * 2 * cbs
    rows = experts * slots * 2 * cbs
    pre = pre_acts.reshape(experts, slots, 2, cbs, 128).transpose(0, 1, 3, 2, 4).reshape(rows, 128)
    code = expert_ids * slots + lax.axis_index("ep") * cap + slot_ids
    table = jnp.concatenate([code.T.astype(jnp.float32), gate_weights.T.astype(jnp.float32)])
    vmem = pl.BlockSpec(memory_space=pltpu.VMEM)
    hbm = pl.BlockSpec(memory_space=pltpu.HBM)
    dma = pltpu.SemaphoreType.DMA
    bf, f32 = jnp.bfloat16, jnp.float32
    out, gg = pl.pallas_call(
        functools.partial(kernel, (experts, slots, cap, hid, chunks)),
        out_shape=(
            jax.ShapeDtypeStruct((rows, 128), bf),
            jax.ShapeDtypeStruct((chosen, 128), f32),
        ),
        in_specs=[hbm, vmem, hbm, hbm],
        out_specs=(vmem, vmem),
        scratch_shapes=[
            pltpu.VMEM((NZ, 2, chunks, NX * 128, KC), bf),
            pltpu.VMEM((2 * chunks, experts, hid, KC), bf),
            pltpu.VMEM((rows, 128), bf),
            pltpu.VMEM((unit, 128), f32),
            pltpu.VMEM((experts, 3, mp, hid), f32),
            pltpu.VMEM((experts, mp, hid), f32),
            pltpu.VMEM((experts, mp, NX * 128), bf),
            pltpu.VMEM((experts, mp, 128), f32),
            pltpu.VMEM((peers, 2 * chosen, 128), f32),
            pltpu.VMEM((NZ, NX, 8, 128), f32),
            pltpu.VMEM((2 * peers, 8, 128), f32),
            dma((peers, chunks)),
            dma((peers, chunks)),
            dma((2, peers)),
            dma((NZ,)),
            dma((peers,)),
            dma((chunks,)),
            dma((2 * chunks,)),
            dma,
            dma((peers,)),
            dma((peers,)),
            dma((NZ, NX, 2)),
            dma((2 * peers,)),
        ],
        compiler_params=pltpu.CompilerParams(
            collective_id=0, has_side_effects=True, vmem_limit_bytes=50 * 2**20
        ),
    )(cotangent, table, pre, w_down)
    grad_pre = (
        out.reshape(experts, slots, cbs, 2, 128)
        .transpose(0, 1, 3, 2, 4)
        .reshape(experts, slots, 2, hid)
    )
    return grad_pre, gg.T


def shards(cotangent, gate_weights, expert_ids, slot_ids, pre_acts, w_down):
    peers = lax.axis_size("ep")
    experts, slots, _, hid = pre_acts.shape
    tokens, chosen = expert_ids.shape
    fits = (
        peers == NZ * NX
        and lax.axis_size("tp") == 2
        and experts * (slots // peers) >= tokens
        and experts <= 8
        and tokens == 128
        and chosen == 8
        and cotangent.shape[1] % KC == 0
        and hid % 128 == 0
    )
    run = relayed if fits else slotted
    return run(cotangent, gate_weights, expert_ids, slot_ids, pre_acts, w_down)


def solution(mesh):
    placed = (
        P(("grp", "ep"), "tp"),
        P(("grp", "ep"), None),
        P(("grp", "ep"), None),
        P(("grp", "ep"), None),
        P("ep", "grp", None, "tp"),
        P("ep", "tp", None),
    )
    return jax.shard_map(
        shards,
        mesh=mesh,
        in_specs=placed,
        out_specs=(P("ep", "grp", None, "tp"), P(("grp", "ep"), None)),
        check_vma=False,
    )
```
